256 devices in a mesh: seq: 64 (over x, y, z_hi, core), head: 4 (over z_lo).
Axes of the slice: x: 4, y: 4, z: 8 (z_hi: 2, z_lo: 4; z = z_hi * 4 + z_lo), core: 2. Of those that a mesh axis runs over, the one named last changes fastest.
Arguments:
- query_nope: bfloat16 [1, 64, 16384], P(None, 'seq', 'head'), may hold values from -6 to 6
- query_rope: bfloat16 [1, 64, 8192], P(None, 'seq', 'head'), may hold values from -8 to 8
- cache_latent: bfloat16 [1, 32768, 512], P(None, ('seq', 'head')), may hold values from -6 to 6
- cache_rope: bfloat16 [1, 32768, 64], P(None, ('seq', 'head')), may hold values from -8 to 8
- key_weight: bfloat16 [128, 128, 512], P('head'), may hold values from -0.5 to 0.5
- value_weight: bfloat16 [128, 512, 128], P('head'), may hold values from -0.25 to 0.25
- span_starts: int32 [1], replicated, may hold values from 32640 to 32704
Outputs:
- attended: bfloat16 [1, 64, 16384], P(None, 'seq', 'head')
The draws below stay inside these ranges and needn't reach their ends.
Inputs may be any that keep to these rules, and one draw needn't show every extreme that they name: `span_starts`: each prompt's new tokens lie inside its cache.
All inputs are finite; a program needn't handle non-finite values.
Results may differ from the reference program's by a relative error of at most 0.0085.
The reference program's roundings to bfloat16 on the way (of `absorbed` and `weights`) count: a program that leaves them out, or rounds other values in their place, can miss the bound.
Values may be sent and summed in bfloat16 or wider, within the bound.
A program may use at most 64 MiB of HBM per device.

```python
import jax
import jax.numpy as jnp
from jax import lax

HEADS = 128
NOPE = 128
ROPE = 64
LATENT = 512
VDIM = 128
PROMPTS = 1
QUERIES = 64
CTX_DEV = 128
CONTEXT = 32768


def draw_cache_rope(key, part):
    key = jax.random.fold_in(key, 7)
    return jnp.clip(jax.random.normal(key, (PROMPTS, CONTEXT, ROPE), jnp.float32), -8.0, 8.0).astype(jnp.bfloat16)


def draw_query_rope(key, part):
    key = jax.random.fold_in(key, 13)
    return jnp.clip(jax.random.normal(key, (PROMPTS, QUERIES, HEADS * ROPE), jnp.float32), -8.0, 8.0).astype(jnp.bfloat16)


def level_of(own_key, dims, split, smallest, top_value):
    factor_of, own = 1.0, jax.random.fold_in(own_key, 6)
    for axis_at, shards_of in split:
        steps = jnp.exp(jax.random.uniform(jax.random.fold_in(own, axis_at), (shards_of,), jnp.float32, smallest / len(split), top_value / len(split)))
        factor_of = factor_of * jnp.repeat(steps, dims[axis_at] // shards_of).reshape([-1 if axis == axis_at else 1 for axis in range(len(dims))])
    return factor_of


def normal_values(own_key, shape, spread, reach, split=(), kind=jnp.bfloat16):
    level = level_of(own_key, shape, split, -0.22, 0.18) if split else 1.0
    drawn = jax.random.normal(own_key, shape, jnp.float32) * spread * level
    return jnp.minimum(jnp.maximum(drawn, -reach), reach).astype(kind)


def setup_inputs(seed: int = 0) -> dict:
    splits = jax.random.split(jax.random.key(seed), 8)
    query_nope = normal_values(splits[0], (PROMPTS, QUERIES, HEADS * NOPE), 1.0, 6.0, ((1, 64), (2, 4)))
    query_rope = draw_query_rope(jax.random.fold_in(splits[7], 71), 0)
    cache_latent = normal_values(splits[2], (PROMPTS, CONTEXT, LATENT), 1.0, 6.0, ((1, 256),))
    cache_rope = draw_cache_rope(jax.random.fold_in(splits[7], 71), 0)
    key_weight = normal_values(splits[4], (HEADS, NOPE, LATENT), NOPE ** -0.5, 0.5, ((0, 4),))
    value_weight = normal_values(splits[5], (HEADS, LATENT, VDIM), LATENT ** -0.5, 0.25, ((0, 4),))
    span_starts = jax.random.randint(splits[6], (PROMPTS,), CONTEXT - QUERIES - CTX_DEV // 2, CONTEXT - QUERIES + 1).astype(jnp.int32)
    return dict(query_nope=query_nope, query_rope=query_rope, cache_latent=cache_latent, cache_rope=cache_rope, key_weight=key_weight, value_weight=value_weight, span_starts=span_starts)


softmax_gain = 0.13524
floor_value = -1.0e30


def reference(query_nope, query_rope, cache_latent, cache_rope, key_weight, value_weight, span_starts):
    nope_parts = query_nope.reshape(PROMPTS, QUERIES, HEADS, NOPE).astype(jnp.float32)
    absorbed = jnp.einsum("bqhd,hdc->bqhc", nope_parts, key_weight.astype(jnp.float32))
    absorbed = lax.optimization_barrier(absorbed.astype(jnp.bfloat16))
    rotary = query_rope.reshape(PROMPTS, QUERIES, HEADS, ROPE)
    limit = span_starts.astype(jnp.int32)[:, None] + jnp.arange(QUERIES, dtype=jnp.int32)[None, :]
    position = jnp.arange(CONTEXT, dtype=jnp.int32)
    visible = position[None, None, :] <= limit[:, :, None]
    latent_full = cache_latent.astype(jnp.float32)
    rope_full = cache_rope.astype(jnp.float32)

    def per_head(operands):
        head_absorbed, head_rotary, head_value = operands
        scores = jnp.einsum("bqc,bpc->bqp", head_absorbed.astype(jnp.float32), latent_full)
        scores = scores + jnp.einsum("bqr,bpr->bqp", head_rotary.astype(jnp.float32), rope_full)
        scores = jnp.where(visible, scores * softmax_gain, floor_value)
        peak = jnp.max(scores, axis=-1, keepdims=True)
        mass = jnp.where(visible, jnp.exp(scores - peak), 0.0)
        denom = jnp.sum(mass, axis=-1)
        weights = lax.optimization_barrier(mass.astype(jnp.bfloat16)).astype(jnp.float32)
        mixed = jnp.einsum("bqp,bpc->bqc", weights, latent_full) / denom[..., None]
        result = jnp.einsum("bqc,cv->bqv", mixed, head_value.astype(jnp.float32), precision=lax.Precision.HIGHEST)
        return result.astype(jnp.bfloat16)

    stacked = lax.map(per_head, (absorbed.transpose(2, 0, 1, 3), rotary.transpose(2, 0, 1, 3), value_weight))
    return stacked.transpose(1, 2, 0, 3).reshape(PROMPTS, QUERIES, HEADS * VDIM)
```

```python
import jax
import jax.numpy as jnp
from jax import lax
from jax.experimental import pallas as pl
from jax.experimental.pallas import tpu as pltpu
from jax.sharding import PartitionSpec as P

MESH = pl.DeviceIdType.MESH
bf16, f32 = jnp.bfloat16, jnp.float32
gain = 0.13524
gain2 = gain * 1.4426950408889634
floor_value = -1e30

HEADS = 16
TOKENS = 32
ROWS = HEADS * TOKENS
BLOCK = 128
PARTS = 3


def coords():
    s, zl = lax.axis_index("seq"), lax.axis_index("head")
    return s // 16, (s // 4) % 4, ((s // 2) % 2) * 4 + zl, s % 2


def device(x, y, z, c):
    return (((x * 4 + y) * 2 + z // 4) * 2 + c, z % 4)


def remote(src, dst, send, recv, to):
    return pltpu.make_async_remote_copy(src, dst, send, recv, device_id=to, device_id_type=MESH)


def kernel(span_ref, qn_hbm, qr_hbm, lat_hbm, rope_hbm, kw_hbm, vw_hbm, out_ref,
           qn, qr, qtmp, qs, rq, qf, kw, vw, lat, rp, rx, rope_own, a_lat, a_rope, m_s, l_s, acc, of, mlf, so, ro,
           load_sem, q_send, q_recv, r_send, r_recv, c_send, c_recv, o_send, o_recv):
    x, y, z, c = coords()
    up, down = device(x, y, (z + 1) % 8, c), device(x, y, (z + 7) % 8, c)
    other = device(x, y, z, 1 - c)
    me = (x * 4 + y) * 2 + c
    peers = []
    for i in range(1, 32):
        dx, dy, dc = i // 8, (i // 2) % 4, i % 2
        px, py, pc = (x + dx) % 4, (y + dy) % 4, (c + dc) % 2
        peers.append((device(px, py, z, pc), (px * 4 + py) * 2 + pc, pc))

    barrier = pltpu.get_barrier_semaphore()
    for to in [p[0] for p in peers] + [up, down]:
        pl.semaphore_signal(barrier, inc=1, device_id=to, device_id_type=MESH)

    my_rows = pl.ds(pl.multiple_of(c * 128, 128), 128)
    loads = [
        pltpu.make_async_copy(qn_hbm, qn, load_sem.at[0]),
        pltpu.make_async_copy(qr_hbm, qr, load_sem.at[1]),
        pltpu.make_async_copy(rope_hbm.at[0], rope_own, load_sem.at[2]),
        pltpu.make_async_copy(lat_hbm.at[0], lat.at[z, my_rows], load_sem.at[3]),
        pltpu.make_async_copy(kw_hbm.at[pl.ds(c * HEADS, HEADS)], kw, load_sem.at[4]),
        pltpu.make_async_copy(vw_hbm.at[pl.ds(c * HEADS, HEADS)], vw, load_sem.at[5]),
    ]
    for copy in loads:
        copy.start()

    lane16 = lax.broadcasted_iota(jnp.int32, (16, 128), 1)
    loads[2].wait()
    eye = lax.broadcasted_iota(jnp.int32, (64, 128), 0) == lax.broadcasted_iota(jnp.int32, (64, 128), 1) % 64
    doubled = jnp.dot(rope_own[...], jnp.where(eye, 1.0, 0.0).astype(bf16), preferred_element_type=f32)
    rope_rows = pl.ds(pl.multiple_of(c * 16, 16), 16)
    for t in range(4):
        tile = jnp.where(lane16 < 64, doubled[32 * t : 32 * t + 16], doubled[32 * t + 16 : 32 * t + 32])
        rp[z, rope_rows, 128 * t : 128 * t + 128] = tile.astype(bf16)
    loads[0].wait()
    loads[1].wait()
    qtmp[...] = jnp.zeros_like(qtmp)
    nope_row, rope_row = qn[0].astype(f32), qr[0].astype(f32)
    for half in range(2):
        for h in range(HEADS):
            at = (half * HEADS + h) * 128
            qtmp[half, h : h + 1, :] = nope_row[:, at : at + 128]
        for h in range(HEADS // 2):
            at = (half * HEADS // 2 + h) * 128
            qtmp[half, 16 + h : 17 + h, :] = rope_row[:, at : at + 128]
    qs[...] = qtmp[...].astype(bf16)
    loads[3].wait()

    pl.semaphore_wait(barrier, 33)

    def part_of(slot, part):
        if part == 2:
            return rp.at[slot, rope_rows]
        return lat.at[slot, pl.ds(pl.multiple_of(c * 128 + 64 * part, 64), 64)]

    sent, ring, paired = [], {}, {}

    def ring_send(d, step, part):
        slot = (z + 8 - step) % 8 if d == 0 else (z + step) % 8
        ref = part_of(slot, part)
        copy = remote(ref, ref, r_send.at[d, step, part], r_recv.at[d, step, part], (up, down)[d])
        copy.start()
        ring[d, step, part] = copy
        sent.append(copy)

    def pair_send(d, step, part):
        slot = (z + 8 - step) % 8 if d == 0 else (z + step) % 8
        ref = part_of(slot, part)
        copy = remote(ref, ref, c_send.at[d, step, part], c_recv.at[d, step, part], other)
        copy.start()
        paired[d, step, part] = copy
        sent.append(copy)

    def ring_event(step, part):
        for d in range(2):
            if (d, step, part) in ring:
                ring[d, step, part].wait_recv()
                if step < 2 or (step == 2 and (d == 0) == (part != 1)):
                    ring_send(d, step + 1, part)
                pair_send(d, step + 1, part)

    for part in range(PARTS):
        for d in range(2):
            ring_send(d, 0, part)
        pair_send(0, 0, part)

    q_copies = []
    for i, (to, _, pc) in enumerate(peers):
        copy = remote(qs.at[pc], rq.at[me], q_send.at[i], q_recv.at[i], to)
        copy.start()
        q_copies.append(copy)
    rq[me] = qs[c]

    for part in range(PARTS):
        ring_event(0, part)

    loads[4].wait()
    for copy in q_copies:
        copy.wait_recv()

    lane_t = lax.broadcasted_iota(jnp.int32, (TOKENS, 128), 1)
    qf[...] = rq[...].reshape(TOKENS * 32, 128).astype(f32)
    for h in range(HEADS):
        rows = slice(h * TOKENS, (h + 1) * TOKENS)
        nope = qf[pl.ds(h, TOKENS, stride=32), :].astype(bf16)
        a_lat[rows, :] = jnp.dot(nope, kw[h], preferred_element_type=f32).astype(bf16)
        rope = qf[pl.ds(16 + h // 2, TOKENS, stride=32), :]
        a_rope[rows, :] = jnp.where((lane_t < 64) == (h % 2 == 0), rope, 0.0).astype(bf16)

    def unpack(slot):
        for cc in range(2):
            for t in range(4):
                tile = rp[slot, cc * 16 : cc * 16 + 16, 128 * t : 128 * t + 128].astype(f32)
                turned = pltpu.roll(tile, 64, 1)
                at = cc * 128 + 32 * t
                rx[slot, at : at + 16, :] = jnp.where(lane16 < 64, tile, turned).astype(bf16)
                rx[slot, at + 16 : at + 32, :] = jnp.where(lane16 < 64, turned, tile).astype(bf16)

    row = lax.broadcasted_iota(jnp.int32, (BLOCK, 128), 0) % TOKENS
    limit = span_ref[0] + (row // 2) * 4 + (z // 4) * 2 + row % 2
    column = lax.broadcasted_iota(jnp.int32, (BLOCK, 128), 1)

    def attend(block, slots, first):
        rows = pl.ds(block * BLOCK, BLOCK)
        tiles = []
        for slot in slots:
            s = lax.dot_general(a_lat[rows, :], lat[slot], (((1,), (1,)), ((), ())), preferred_element_type=f32)
            s += lax.dot_general(a_rope[rows, :], rx[slot], (((1,), (1,)), ((), ())), preferred_element_type=f32)
            for cc in range(2):
                base = ((((x * 4 + y) * 2 + slot // 4) * 2 + cc) * 4 + slot % 4) * 128
                tiles.append(jnp.where(column + base <= limit, s[:, cc * 128 : cc * 128 + 128], floor_value))
        top = tiles[0]
        for tile in tiles[1:]:
            top = jnp.maximum(top, tile)
        top = jnp.broadcast_to(jnp.max(top, axis=1, keepdims=True), (BLOCK, 128))
        if not first:
            before = m_s[rows, :]
            top = jnp.maximum(top, before)
            keep = jnp.exp2((before - top) * gain2)
        mass = [jnp.exp2((tile - top) * gain2) for tile in tiles]
        total = mass[0]
        for tile in mass[1:]:
            total = total + tile
        total = jnp.broadcast_to(jnp.sum(total, axis=1, keepdims=True), (BLOCK, 128))
        update = None
        for i, slot in enumerate(slots):
            weights = jnp.concatenate(mass[2 * i : 2 * i + 2], axis=1).astype(bf16)
            term = jnp.dot(weights, lat[slot], preferred_element_type=f32)
            update = term if update is None else update + term
        m_s[rows, :] = top
        if first:
            l_s[rows, :] = total
            acc[rows, :] = update
        else:
            l_s[rows, :] = l_s[rows, :] * keep + total
            for t in range(4):
                acc[rows, 128 * t : 128 * t + 128] = acc[rows, 128 * t : 128 * t + 128] * keep + update[:, 128 * t : 128 * t + 128]

    for step in range(5):
        if step in (0, 4):
            slots = [(z + step) % 8]
        else:
            slots = [(z + 8 - step) % 8, (z + step) % 8]
        for (d, s, part), copy in paired.items():
            if s == step:
                copy.wait_recv()
        for slot in slots:
            unpack(slot)
        for block in range(ROWS // BLOCK):
            attend(block, slots, step == 0)
            if block < PARTS and step < 3:
                ring_event(step + 1, block)

    loads[5].wait()
    lane = lax.broadcasted_iota(jnp.int32, (TOKENS, 128), 1)

    def split3(v):
        hi = v.astype(bf16).astype(f32)
        mid = (v - hi).astype(bf16).astype(f32)
        return hi, mid, v - hi - mid

    for h in range(HEADS):
        rows = slice(h * TOKENS, (h + 1) * TOKENS)
        of[pl.ds(h, TOKENS, stride=HEADS), :] = jnp.dot(acc[rows, :].astype(bf16), vw[h], preferred_element_type=f32)
        values = split3(m_s[rows, :]) + split3(l_s[rows, :])
        packed = jnp.zeros((TOKENS, 128), f32)
        for i, v in enumerate(values):
            packed = jnp.where(lane == i, v, packed)
        mlf[pl.ds(h, TOKENS, stride=HEADS), :] = packed
    so[:, 0:16, :] = of[...].reshape(TOKENS, HEADS, 128).astype(bf16)
    so[:, 16:32, :] = mlf[...].reshape(TOKENS, HEADS, 128).astype(bf16)
    o_copies = []
    for i, (to, token, _) in enumerate(peers):
        copy = remote(so.at[token], ro.at[me], o_send.at[i], o_recv.at[i], to)
        copy.start()
        o_copies.append(copy)
    ro[me] = so[me]
    for copy in o_copies:
        copy.wait_recv()

    for half in range(2):
        tops, sums = [], []
        for p in range(16):
            ml = ro[2 * p + half, 16:32, :].astype(f32)
            tops.append(jnp.sum(jnp.where(lane16 < 3, ml, 0.0), axis=1, keepdims=True))
            sums.append(jnp.sum(jnp.where((lane16 >= 3) & (lane16 < 6), ml, 0.0), axis=1, keepdims=True))
        top = tops[0]
        for t in tops[1:]:
            top = jnp.maximum(top, t)
        num, den = jnp.zeros((16, 128), f32), jnp.zeros((16, 1), f32)
        for p in range(16):
            scale = jnp.exp2((tops[p] - top) * gain2)
            num += scale * ro[2 * p + half, 0:16, :].astype(f32)
            den += scale * sums[p]
        out_ref[half * 16 : half * 16 + 16, :] = (num / den).astype(bf16)

    for copy in sent + q_copies + o_copies:
        copy.wait_send()


def body(query_nope, query_rope, cache_latent, cache_rope, key_weight, value_weight, span_starts):
    dma = pltpu.SemaphoreType.DMA
    vmem = pltpu.VMEM
    out = pl.pallas_call(
        kernel,
        out_shape=jax.ShapeDtypeStruct((32, 128), bf16),
        in_specs=[pl.BlockSpec(memory_space=pltpu.SMEM)] + [pl.BlockSpec(memory_space=pl.ANY)] * 6,
        out_specs=pl.BlockSpec(memory_space=pltpu.VMEM),
        scratch_shapes=[
            vmem((1, 1, 4096), bf16), vmem((1, 1, 2048), bf16), vmem((2, 32, 128), f32), vmem((2, 32, 128), bf16),
            vmem((32, 32, 128), bf16), vmem((1024, 128), f32), vmem((HEADS, 128, 512), bf16), vmem((HEADS, 512, 128), bf16),
            vmem((8, 256, 512), bf16), vmem((8, 32, 512), bf16), vmem((8, 256, 128), bf16), vmem((128, 64), bf16),
            vmem((ROWS, 512), bf16), vmem((ROWS, 128), bf16), vmem((ROWS, 128), f32), vmem((ROWS, 128), f32),
            vmem((ROWS, 512), f32), vmem((ROWS, 128), f32), vmem((ROWS, 128), f32),
            vmem((32, 32, 128), bf16), vmem((32, 32, 128), bf16),
            dma((6,)), dma((31,)), dma((31,)), dma((2, 4, PARTS)), dma((2, 4, PARTS)),
            dma((2, 5, PARTS)), dma((2, 5, PARTS)), dma((31,)), dma((31,)),
        ],
        compiler_params=pltpu.CompilerParams(collective_id=0, has_side_effects=True, vmem_limit_bytes=40 << 20),
        cost_estimate=pl.CostEstimate(flops=2 * 512 * 2048 * 1152, bytes_accessed=5 << 20, transcendentals=1 << 20),
    )(span_starts, query_nope, query_rope, cache_latent, cache_rope, key_weight, value_weight)
    return out.reshape(1, 1, 4096)


def solution(mesh):
    placed = (
        P(None, "seq", "head"),
        P(None, "seq", "head"),
        P(None, ("seq", "head"), None),
        P(None, ("seq", "head"), None),
        P("head", None, None),
        P("head", None, None),
        P(),
    )
    return jax.shard_map(
        body, mesh=mesh, in_specs=placed, out_specs=P(None, "seq", "head"), check_vma=False
    )
```

```python
import jax
import jax.numpy as jnp
from jax import lax
from jax.experimental import pallas as pl
from jax.experimental.pallas import tpu as pltpu
from jax.sharding import PartitionSpec as P

MESH = pl.DeviceIdType.MESH
bf16, f32 = jnp.bfloat16, jnp.float32
gain = 0.13524
gain2 = gain * 1.4426950408889634
floor_value = -1e30

HEADS = 16
TOKENS = 32
SIDE = HEADS * TOKENS
BLOCK = 128
PARTS = 3
ORDER = sorted(
    ((dx, dy) for dx in range(4) for dy in range(4) if dx or dy), key=lambda d: -min(d[0], 4 - d[0]) - min(d[1], 4 - d[1])
)


def coords():
    s, zl = lax.axis_index("seq"), lax.axis_index("head")
    return s // 16, (s // 4) % 4, ((s // 2) % 2) * 4 + zl, s % 2


def device(x, y, z, c):
    return (((x * 4 + y) * 2 + z // 4) * 2 + c, z % 4)


def remote(src, dst, send, recv, to):
    return pltpu.make_async_remote_copy(src, dst, send, recv, device_id=to, device_id_type=MESH)


def split3(v):
    hi = v.astype(bf16).astype(f32)
    mid = (v - hi).astype(bf16).astype(f32)
    return hi, mid, v - hi - mid


def pack_stats(stats):
    lane = lax.broadcasted_iota(jnp.int32, (16, 128), 1)
    packed = jnp.zeros((16, 128), f32)
    for i, v in enumerate(part for stat in stats for part in split3(stat)):
        packed = jnp.where(lane == i, v, packed)
    return packed


def merge(parts):
    lane = lax.broadcasted_iota(jnp.int32, (16, 128), 1)
    tops, totals = [], []
    for _, stats, at in parts:
        stats = stats.astype(f32)
        tops.append(jnp.sum(jnp.where((lane >= at) & (lane < at + 3), stats, 0.0), axis=1, keepdims=True))
        totals.append(jnp.sum(jnp.where((lane >= at + 3) & (lane < at + 6), stats, 0.0), axis=1, keepdims=True))
    top = tops[0]
    for t in tops[1:]:
        top = jnp.maximum(top, t)
    num, den = jnp.zeros((16, 128), f32), jnp.zeros((16, 1), f32)
    for (sums, _, _), t, total in zip(parts, tops, totals):
        scale = jnp.exp2((t - top) * gain2)
        num += scale * sums.astype(f32)
        den += scale * total
    return num, top, den


def kernel(span_ref, qn_hbm, qr_hbm, lat_hbm, rope_hbm, kw_hbm, vw_hbm, out_ref,
           qn, qr, qtmp, qs, qc, qm, rq, qf, kw, vw, lat, rp, rx, a_lat, a_rope, m_s, l_s, acc, of, so, ro, mm, fin,
           load_sem, q_send, q_recv, z_send, z_recv, f_send, f_recv, r_send, r_recv, c_send, c_recv, o_send, o_recv):
    x, y, z, c = coords()
    up, down = device(x, y, (z + 1) % 8, c), device(x, y, (z + 7) % 8, c)
    onward = device(x, y, (z + 1 + 6 * c) % 8, c)
    far = [device(x, y, (z + 4) % 8, c), device(x, y, (z + 4) % 8, 1 - c)]
    other = device(x, y, z, 1 - c)
    me = x * 4 + y
    peers = []
    for dx, dy in ORDER:
        px, py = (x + dx) % 4, (y + dy) % 4
        peers.append((device(px, py, z, c), px * 4 + py))

    rows_of = pl.ds(pl.multiple_of(c * 128, 128), 128)
    loads = [
        pltpu.make_async_copy(qn_hbm, qn, load_sem.at[0]),
        pltpu.make_async_copy(qr_hbm, qr, load_sem.at[1]),
        pltpu.make_async_copy(rope_hbm.at[0], rp.at[0, c], load_sem.at[2]),
        pltpu.make_async_copy(lat_hbm.at[0], lat.at[0, rows_of], load_sem.at[3]),
        pltpu.make_async_copy(kw_hbm.at[pl.ds(c * HEADS, HEADS)], kw, load_sem.at[4]),
        pltpu.make_async_copy(vw_hbm.at[pl.ds(c * HEADS, HEADS)], vw, load_sem.at[5]),
    ]
    for copy in loads:
        copy.start()

    barrier = pltpu.get_barrier_semaphore()
    for to in far + [up, down, other] + [p[0] for p in peers]:
        pl.semaphore_signal(barrier, inc=1, device_id=to, device_id_type=MESH)

    loads[0].wait()
    loads[1].wait()
    qtmp[...] = jnp.zeros_like(qtmp)
    nope_row, rope_row = qn[0].astype(f32), qr[0].astype(f32)
    for half in range(2):
        for h in range(HEADS):
            at = (half * HEADS + h) * 128
            qtmp[half, h : h + 1, :] = nope_row[:, at : at + 128]
        for h in range(HEADS // 2):
            at = (half * HEADS // 2 + h) * 128
            qtmp[half, pl.ds(16 + 8 * c + h, 1), :] = rope_row[:, at : at + 128]
    qs[...] = qtmp[...].astype(bf16)
    loads[2].wait()
    loads[3].wait()

    pl.semaphore_wait(barrier, 20)

    started = []

    def start(copy):
        copy.start()
        started.append(copy)
        return copy

    def piece(slot, part):
        if part == 2:
            return rp.at[slot, c]
        return lat.at[slot, pl.ds(pl.multiple_of(c * 128 + 64 * part, 64), 64)]

    def pair(slot, part):
        ref = piece(slot, part)
        return start(remote(ref, ref, c_send.at[slot, part], c_recv.at[slot, part], other))

    to_far = [
        start(remote(qs.at[c], qc.at[1, c], z_send.at[0], z_recv.at[0], far[0])),
        start(remote(qs.at[1 - c], qc.at[1, c], z_send.at[1], z_recv.at[1], far[1])),
    ]
    to_other = start(remote(qs.at[1 - c], qc.at[0, c], z_send.at[2], z_recv.at[2], other))
    qc[0, c] = qs[c]
    hop1, hop2, paired = {}, {}, []
    for part in range(PARTS):
        for d, to in enumerate((up, down)):
            hop1[d, part] = start(
                remote(piece(0, part), piece(1 + d, part), r_send.at[d, part], r_recv.at[d, part], to)
            )

    def send_queries(side):
        for core in range(2):
            qm[side, core] = qc[side, core, 0:16, :]
        qm[side, 2] = qc[side, 0, 16:32, :] + qc[side, 1, 16:32, :]
        copies = []
        for i, (to, _) in enumerate(peers):
            copies.append(start(remote(qm.at[side], rq.at[side, me], q_send.at[side, i], q_recv.at[side, i], to)))
        rq[side, me] = qm[side]
        return copies

    for part in range(PARTS):
        paired.append(pair(0, part))
    to_other.wait_recv()
    own_queries = send_queries(0)

    def arrive(part):
        for d in range(2):
            hop1[d, part].wait_recv()
        hop2[part] = start(
            remote(piece(1 + c, part), piece(3, part), r_send.at[2, part], r_recv.at[2, part], onward)
        )
        for d in range(2):
            paired.append(pair(1 + d, part))

    for copy in to_far:
        copy.wait_recv()
    far_queries = send_queries(1)
    for part in range(PARTS):
        arrive(part)

    lane_t = lax.broadcasted_iota(jnp.int32, (TOKENS, 128), 1)

    def by_head(row):
        return [qf[pl.ds(row[core], 16, stride=48), :] for core in range(2)]

    def absorb(side):
        qf[...] = rq[side].reshape(16 * 48, 128).astype(f32)
        for h in range(HEADS):
            rows = slice(side * SIDE + h * TOKENS, side * SIDE + (h + 1) * TOKENS)
            nope = jnp.concatenate(by_head((h, 16 + h)), axis=0).astype(bf16)
            a_lat[rows, :] = jnp.dot(nope, kw[h], preferred_element_type=f32).astype(bf16)
            rope = jnp.concatenate(by_head((32 + h // 2, 40 + h // 2)), axis=0)
            a_rope[rows, :] = jnp.where((lane_t < 64) == (h % 2 == 0), rope, 0.0).astype(bf16)

    def double_keys(slot):
        for cc in range(2):
            for twice in range(2):
                at = 256 * slot + 128 * cc
                rx[64 * twice : 64 * twice + 64, at : at + 128] = rp[slot, cc]

    row = lax.broadcasted_iota(jnp.int32, (BLOCK, 128), 0) % TOKENS
    column = lax.broadcasted_iota(jnp.int32, (BLOCK, 128), 1)

    def attend(side, block, low, high, first):
        rows = pl.ds(side * SIDE + block * BLOCK, BLOCK)
        z_hi = (z // 4 + side) % 2
        limit = span_ref[0] + (row % 16) * 4 + z_hi * 2 + row // 16 - column
        keys = lat[low:high].reshape((high - low) * 256, 512)
        s = lax.dot_general(a_lat[rows, :], keys, (((1,), (1,)), ((), ())), preferred_element_type=f32)
        s += jnp.dot(a_rope[rows, :], rx[:, 256 * low : 256 * high], preferred_element_type=f32)
        tiles = []
        for slot in range(low, high):
            for cc in range(2):
                zz = (z + (0, 7, 1, (6, 2)[cc])[slot]) % 8
                base = ((((x * 4 + y) * 2 + zz // 4) * 2 + cc) * 4 + zz % 4) * 128
                at = 128 * len(tiles)
                tiles.append(jnp.where(limit >= base, s[:, at : at + 128], floor_value))
        top = tiles[0]
        for tile in tiles[1:]:
            top = jnp.maximum(top, tile)
        top = jnp.broadcast_to(jnp.max(top, axis=1, keepdims=True), (BLOCK, 128))
        if not first:
            before = m_s[rows, :]
            top = jnp.maximum(top, before)
            keep = jnp.exp2((before - top) * gain2)
        mass = [jnp.exp2((tile - top) * gain2) for tile in tiles]
        total = mass[0]
        for tile in mass[1:]:
            total = total + tile
        total = jnp.broadcast_to(jnp.sum(total, axis=1, keepdims=True), (BLOCK, 128))
        update = jnp.dot(jnp.concatenate(mass, axis=1).astype(bf16), keys, preferred_element_type=f32)
        m_s[rows, :] = top
        if first:
            l_s[rows, :] = total
            acc[rows, :] = update
        else:
            l_s[rows, :] = l_s[rows, :] * keep + total
            for t in range(4):
                at = slice(128 * t, 128 * t + 128)
                acc[rows, at] = acc[rows, at] * keep + update[:, at]

    def send_partials(side):
        for h in range(HEADS):
            rows = slice(side * SIDE + h * TOKENS, side * SIDE + (h + 1) * TOKENS)
            result = jnp.dot(acc[rows, :].astype(bf16), vw[h], preferred_element_type=f32)
            stats = []
            for core in range(2):
                of[pl.ds(16 * core + h, 16, stride=48), :] = result[16 * core : 16 * core + 16]
                at = slice(rows.start + 16 * core, rows.start + 16 * core + 16)
                stats += [m_s[at, :], l_s[at, :]]
            of[pl.ds(32 + h, 16, stride=48), :] = pack_stats(stats)
        so[side] = of[...].reshape(16, 48, 128).astype(bf16)
        copies = []
        for i, (to, p) in enumerate(peers):
            copies.append(
                start(remote(so.at[side, p], ro.at[side, me], o_send.at[side, i], o_recv.at[side, i], to))
            )
        ro[side, me] = so[side, me]
        return copies

    loads[4].wait()
    for copy in own_queries:
        copy.wait_recv()
    absorb(0)
    for copy in paired:
        copy.wait_recv()
    for slot in range(3):
        double_keys(slot)
    for block in range(SIDE // BLOCK):
        attend(0, block, 0, 3, True)

    last = []
    for part in range(PARTS):
        hop2[part].wait_recv()
        last.append(pair(3, part))
    for copy in far_queries:
        copy.wait_recv()
    absorb(1)
    for block in range(SIDE // BLOCK):
        attend(1, block, 0, 3, True)
    for copy in last:
        copy.wait_recv()
    double_keys(3)
    for block in range(SIDE // BLOCK):
        attend(1, block, 3, 4, False)
    loads[5].wait()
    far_partials = send_partials(1)
    for block in range(SIDE // BLOCK):
        attend(0, block, 3, 4, False)
    own_partials = send_partials(0)

    def merge_plane(side):
        for core in range(2):
            num, top, den = merge(
                [(ro[side, p, 16 * core : 16 * core + 16, :], ro[side, p, 32:48, :], 6 * core) for p in range(16)]
            )
            mm[side, core, 0:16, :] = num.astype(bf16)
            mm[side, core, 16:32, :] = pack_stats([top, den]).astype(bf16)

    for copy in far_partials:
        copy.wait_recv()
    merge_plane(1)
    finals = [
        start(remote(mm.at[1, c], fin.at[1, c], f_send.at[0], f_recv.at[0], far[0])),
        start(remote(mm.at[1, 1 - c], fin.at[1, c], f_send.at[1], f_recv.at[1], far[1])),
    ]
    for copy in own_partials:
        copy.wait_recv()
    merge_plane(0)
    finals.append(start(remote(mm.at[0, 1 - c], fin.at[0, c], f_send.at[2], f_recv.at[2], other)))
    fin[0, c] = mm[0, c]
    for copy in finals:
        copy.wait_recv()
    for half in range(2):
        num, _, den = merge([(fin[source, half, 0:16, :], fin[source, half, 16:32, :], 0) for source in range(2)])
        out_ref[half * 16 : half * 16 + 16, :] = (num / den).astype(bf16)

    for copy in started:
        copy.wait_send()


def body(query_nope, query_rope, cache_latent, cache_rope, key_weight, value_weight, span_starts):
    dma = pltpu.SemaphoreType.DMA
    vmem = pltpu.VMEM
    out = pl.pallas_call(
        kernel,
        out_shape=pltpu.VMEM((32, 128), bf16),
        in_specs=[pl.BlockSpec(memory_space=pltpu.SMEM)] + [pl.BlockSpec(memory_space=pl.ANY)] * 6,
        out_specs=pl.BlockSpec(memory_space=pltpu.VMEM),
        scratch_shapes=[
            vmem((1, 1, 4096), bf16), vmem((1, 1, 2048), bf16), vmem((2, 32, 128), f32), vmem((2, 32, 128), bf16),
            vmem((2, 2, 32, 128), bf16), vmem((2, 3, 16, 128), bf16), vmem((2, 16, 3, 16, 128), bf16), vmem((768, 128), f32),
            vmem((HEADS, 128, 512), bf16), vmem((HEADS, 512, 128), bf16),
            vmem((4, 256, 512), bf16), vmem((4, 2, 64, 128), bf16), vmem((128, 1024), bf16),
            vmem((2 * SIDE, 512), bf16), vmem((2 * SIDE, 128), bf16), vmem((2 * SIDE, 128), f32), vmem((2 * SIDE, 128), f32),
            vmem((2 * SIDE, 512), f32), vmem((768, 128), f32),
            vmem((2, 16, 48, 128), bf16), vmem((2, 16, 48, 128), bf16), vmem((2, 2, 32, 128), bf16), vmem((2, 2, 32, 128), bf16),
            dma((6,)), dma((2, 15)), dma((2, 15)), dma((3,)), dma((3,)), dma((3,)), dma((3,)), dma((3, PARTS)), dma((3, PARTS)),
            dma((4, PARTS)), dma((4, PARTS)), dma((2, 15)), dma((2, 15)),
        ],
        compiler_params=pltpu.CompilerParams(collective_id=0, has_side_effects=True, vmem_limit_bytes=63 << 20),
        cost_estimate=pl.CostEstimate(flops=2 * 1024 * 1024 * 1152, bytes_accessed=5 << 20, transcendentals=1 << 20),
    )(span_starts, query_nope, query_rope, cache_latent, jnp.swapaxes(cache_rope, 1, 2), key_weight, value_weight)
    return out.reshape(1, 1, 4096)


def solution(mesh):
    placed = (
        P(None, "seq", "head"),
        P(None, "seq", "head"),
        P(None, ("seq", "head"), None),
        P(None, ("seq", "head"), None),
        P("head", None, None),
        P("head", None, None),
        P(),
    )
    return jax.shard_map(
        body, mesh=mesh, in_specs=placed, out_specs=P(None, "seq", "head"), check_vma=False
    )
```

```python
import jax
import jax.numpy as jnp
from jax import lax
from jax.experimental import pallas as pl
from jax.experimental.pallas import tpu as pltpu
from jax.sharding import PartitionSpec as P

MESH = pl.DeviceIdType.MESH
bf16, f32 = jnp.bfloat16, jnp.float32
gain = 0.13524
gain2 = gain * 1.4426950408889634
floor_value = -1e30

HEADS = 16
TOKENS = 32
SIDE = HEADS * TOKENS
BLOCK = 512
PARTS = 3
ORDER = sorted(
    ((dx, dy) for dx in range(4) for dy in range(4) if dx or dy), key=lambda d: -min(d[0], 4 - d[0]) - min(d[1], 4 - d[1])
)


def coords():
    s, zl = lax.axis_index("seq"), lax.axis_index("head")
    return s // 16, (s // 4) % 4, ((s // 2) % 2) * 4 + zl, s % 2


def device(x, y, z, c):
    return (((x * 4 + y) * 2 + z // 4) * 2 + c, z % 4)


def remote(src, dst, send, recv, to):
    return pltpu.make_async_remote_copy(src, dst, send, recv, device_id=to, device_id_type=MESH)


def split3(v):
    hi = v.astype(bf16).astype(f32)
    mid = (v - hi).astype(bf16).astype(f32)
    return hi, mid, v - hi - mid


def pack_stats(stats):
    lane = lax.broadcasted_iota(jnp.int32, (16, 128), 1)
    packed = jnp.zeros((16, 128), f32)
    for i, v in enumerate(part for stat in stats for part in split3(stat)):
        packed = jnp.where(lane == i, v, packed)
    return packed


def merge(parts):
    lane = lax.broadcasted_iota(jnp.int32, (16, 128), 1)
    tops, totals = [], []
    for _, stats, at in parts:
        stats = stats.astype(f32)
        tops.append(jnp.sum(jnp.where((lane >= at) & (lane < at + 3), stats, 0.0), axis=1, keepdims=True))
        totals.append(jnp.sum(jnp.where((lane >= at + 3) & (lane < at + 6), stats, 0.0), axis=1, keepdims=True))
    top = tops[0]
    for t in tops[1:]:
        top = jnp.maximum(top, t)
    num, den = jnp.zeros((16, 128), f32), jnp.zeros((16, 1), f32)
    for (sums, _, _), t, total in zip(parts, tops, totals):
        scale = jnp.exp2((t - top) * gain2)
        num += scale * sums.astype(f32)
        den += scale * total
    return num, top, den


def kernel(span_ref, qn_hbm, qr_hbm, lat_hbm, rope_hbm, kw_hbm, vw_hbm, out_ref,
           qn, qr, qtmp, qs, qc, qm, rq, qf, kw, vw, lat, rp, rx, a_lat, a_rope, m_s, l_s, acc, of, so, ro, mm, fin,
           load_sem, q_send, q_recv, z_send, z_recv, f_send, f_recv, r_send, r_recv, c_send, c_recv, o_send, o_recv):
    x, y, z, c = coords()
    up, down = device(x, y, (z + 1) % 8, c), device(x, y, (z + 7) % 8, c)
    far = [device(x, y, (z + 4) % 8, c), device(x, y, (z + 4) % 8, 1 - c)]
    other = device(x, y, z, 1 - c)
    me = x * 4 + y
    peers = []
    for dx, dy in ORDER:
        px, py = (x + dx) % 4, (y + dy) % 4
        peers.append((device(px, py, z, c), px * 4 + py))

    barrier = pltpu.get_barrier_semaphore()
    for to in far + [up, down, other] + [p[0] for p in peers]:
        pl.semaphore_signal(barrier, inc=1, device_id=to, device_id_type=MESH)

    rows_of = pl.ds(pl.multiple_of(c * 128, 128), 128)
    loads = [
        pltpu.make_async_copy(qn_hbm, qn, load_sem.at[0]),
        pltpu.make_async_copy(qr_hbm, qr, load_sem.at[1]),
        pltpu.make_async_copy(rope_hbm.at[0], rp.at[0, c], load_sem.at[2]),
        pltpu.make_async_copy(lat_hbm.at[0], lat.at[0, rows_of], load_sem.at[3]),
        pltpu.make_async_copy(kw_hbm.at[pl.ds(c * HEADS, HEADS)], kw, load_sem.at[4]),
        pltpu.make_async_copy(vw_hbm.at[pl.ds(c * HEADS, HEADS)], vw, load_sem.at[5]),
    ]
    for copy in loads:
        copy.start()

    loads[0].wait()
    loads[1].wait()
    qtmp[...] = jnp.zeros_like(qtmp)
    nope_row, rope_row = qn[0].astype(f32), qr[0].astype(f32)
    for half in range(2):
        for h in range(HEADS):
            at = (half * HEADS + h) * 128
            qtmp[half, h : h + 1, :] = nope_row[:, at : at + 128]
        for h in range(HEADS // 2):
            at = (half * HEADS // 2 + h) * 128
            qtmp[half, pl.ds(16 + 8 * c + h, 1), :] = rope_row[:, at : at + 128]
    qs[...] = qtmp[...].astype(bf16)
    loads[2].wait()
    loads[3].wait()

    pl.semaphore_wait(barrier, 20)

    started = []

    def start(copy):
        copy.start()
        started.append(copy)
        return copy

    def piece(slot, part):
        if part == 2:
            return rp.at[slot, c]
        return lat.at[slot, pl.ds(pl.multiple_of(c * 128 + 64 * part, 64), 64)]

    def pair(slot, part):
        ref = piece(slot, part)
        return start(remote(ref, ref, c_send.at[slot, part], c_recv.at[slot, part], other))

    to_far = [
        start(remote(qs.at[c], qc.at[1, c], z_send.at[0], z_recv.at[0], far[0])),
        start(remote(qs.at[1 - c], qc.at[1, c], z_send.at[1], z_recv.at[1], far[1])),
    ]
    to_other = start(remote(qs.at[1 - c], qc.at[0, c], z_send.at[2], z_recv.at[2], other))
    qc[0, c] = qs[c]
    hop1, hop2, paired = {}, {}, []
    for part in range(PARTS):
        for d, to in enumerate((up, down)):
            hop1[d, part] = start(
                remote(piece(0, part), piece(1 + d, part), r_send.at[d, part], r_recv.at[d, part], to)
            )

    def send_queries(side):
        for core in range(2):
            qm[side, core] = qc[side, core, 0:16, :]
        qm[side, 2] = qc[side, 0, 16:32, :] + qc[side, 1, 16:32, :]
        copies = []
        for i, (to, _) in enumerate(peers):
            copies.append(start(remote(qm.at[side], rq.at[side, me], q_send.at[side, i], q_recv.at[side, i], to)))
        rq[side, me] = qm[side]
        return copies

    for part in range(PARTS):
        paired.append(pair(0, part))
    to_other.wait_recv()
    own_queries = send_queries(0)

    def arrive(part):
        for d in range(2):
            hop1[d, part].wait_recv()
            hop2[d, part] = start(
                remote(piece(1 + d, part), piece(3 + d, part), r_send.at[2 + d, part], r_recv.at[2 + d, part], (up, down)[d])
            )
        for d in range(2):
            paired.append(pair(1 + d, part))

    for copy in to_far:
        copy.wait_recv()
    far_queries = send_queries(1)
    for part in range(PARTS):
        arrive(part)

    lane_t = lax.broadcasted_iota(jnp.int32, (TOKENS, 128), 1)

    def by_head(row):
        return [qf[pl.ds(row[core], 16, stride=48), :] for core in range(2)]

    def absorb(side):
        qf[...] = rq[side].reshape(16 * 48, 128).astype(f32)
        for h in range(HEADS):
            rows = slice(side * SIDE + h * TOKENS, side * SIDE + (h + 1) * TOKENS)
            nope = jnp.concatenate(by_head((h, 16 + h)), axis=0).astype(bf16)
            a_lat[rows, :] = jnp.dot(nope, kw[h], preferred_element_type=f32).astype(bf16)
            rope = jnp.concatenate(by_head((32 + h // 2, 40 + h // 2)), axis=0)
            a_rope[rows, :] = jnp.where((lane_t < 64) == (h % 2 == 0), rope, 0.0).astype(bf16)

    def double_keys(slot):
        for cc in range(2):
            for twice in range(2):
                at = 256 * slot + 128 * cc
                rx[64 * twice : 64 * twice + 64, at : at + 128] = rp[slot, cc]

    row = lax.broadcasted_iota(jnp.int32, (BLOCK, 128), 0) % TOKENS
    column = lax.broadcasted_iota(jnp.int32, (BLOCK, 128), 1)

    def attend(side, block, low, high, first):
        rows = pl.ds(side * SIDE + block * BLOCK, BLOCK)
        z_hi = (z // 4 + side) % 2
        limit = span_ref[0] + (row % 16) * 4 + z_hi * 2 + row // 16 - column
        keys = lat[low:high].reshape((high - low) * 256, 512)
        s = lax.dot_general(a_lat[rows, :], keys, (((1,), (1,)), ((), ())), preferred_element_type=f32)
        s += jnp.dot(a_rope[rows, :], rx[:, 256 * low : 256 * high], preferred_element_type=f32)
        tiles = []
        for slot in range(low, high):
            for cc in range(2):
                zz = (z + (0, 7, 1, 6, 2)[slot]) % 8
                base = ((((x * 4 + y) * 2 + zz // 4) * 2 + cc) * 4 + zz % 4) * 128
                at = 128 * len(tiles)
                tiles.append(jnp.where(limit >= base, s[:, at : at + 128], floor_value))
        top = tiles[0]
        for tile in tiles[1:]:
            top = jnp.maximum(top, tile)
        top = jnp.broadcast_to(jnp.max(top, axis=1, keepdims=True), (BLOCK, 128))
        if not first:
            before = m_s[rows, :]
            top = jnp.maximum(top, before)
            keep = jnp.exp2((before - top) * gain2)
        mass = [jnp.exp2((tile - top) * gain2) for tile in tiles]
        total = mass[0]
        for tile in mass[1:]:
            total = total + tile
        total = jnp.broadcast_to(jnp.sum(total, axis=1, keepdims=True), (BLOCK, 128))
        update = jnp.dot(jnp.concatenate(mass, axis=1).astype(bf16), keys, preferred_element_type=f32)
        m_s[rows, :] = top
        if first:
            l_s[rows, :] = total
            acc[rows, :] = update
        else:
            l_s[rows, :] = l_s[rows, :] * keep + total
            for t in range(4):
                at = slice(128 * t, 128 * t + 128)
                acc[rows, at] = acc[rows, at] * keep + update[:, at]

    def send_partials(side):
        for h in range(HEADS):
            rows = slice(side * SIDE + h * TOKENS, side * SIDE + (h + 1) * TOKENS)
            result = jnp.dot(acc[rows, :].astype(bf16), vw[h], preferred_element_type=f32)
            stats = []
            for core in range(2):
                of[pl.ds(16 * core + h, 16, stride=48), :] = result[16 * core : 16 * core + 16]
                at = slice(rows.start + 16 * core, rows.start + 16 * core + 16)
                stats += [m_s[at, :], l_s[at, :]]
            of[pl.ds(32 + h, 16, stride=48), :] = pack_stats(stats)
        so[side] = of[...].reshape(16, 48, 128).astype(bf16)
        copies = []
        for i, (to, p) in enumerate(peers):
            copies.append(
                start(remote(so.at[side, p], ro.at[side, me], o_send.at[side, i], o_recv.at[side, i], to))
            )
        ro[side, me] = so[side, me]
        return copies

    loads[4].wait()
    for copy in own_queries:
        copy.wait_recv()
    absorb(0)
    for copy in paired:
        copy.wait_recv()
    for slot in range(3):
        double_keys(slot)
    for block in range(SIDE // BLOCK):
        attend(0, block, 0, 3, True)

    for copy in far_queries:
        copy.wait_recv()
    absorb(1)
    for block in range(SIDE // BLOCK):
        attend(1, block, 0, 3, True)
    loads[5].wait()
    far_partials = send_partials(1)
    last = []
    for part in range(PARTS):
        for d in range(2):
            hop2[d, part].wait_recv()
            last.append(pair(3 + d, part))
    for copy in last:
        copy.wait_recv()
    for slot in (3, 4):
        double_keys(slot)
    for block in range(SIDE // BLOCK):
        attend(0, block, 3, 5, False)
    own_partials = send_partials(0)

    def merge_plane(side):
        for core in range(2):
            num, top, den = merge(
                [(ro[side, p, 16 * core : 16 * core + 16, :], ro[side, p, 32:48, :], 6 * core) for p in range(16)]
            )
            mm[side, core, 0:16, :] = num.astype(bf16)
            mm[side, core, 16:32, :] = pack_stats([top, den]).astype(bf16)

    for copy in far_partials:
        copy.wait_recv()
    merge_plane(1)
    finals = [
        start(remote(mm.at[1, c], fin.at[1, c], f_send.at[0], f_recv.at[0], far[0])),
        start(remote(mm.at[1, 1 - c], fin.at[1, c], f_send.at[1], f_recv.at[1], far[1])),
    ]
    for copy in own_partials:
        copy.wait_recv()
    merge_plane(0)
    finals.append(start(remote(mm.at[0, 1 - c], fin.at[0, c], f_send.at[2], f_recv.at[2], other)))
    fin[0, c] = mm[0, c]
    for copy in finals:
        copy.wait_recv()
    for half in range(2):
        num, _, den = merge([(fin[source, half, 0:16, :], fin[source, half, 16:32, :], 0) for source in range(2)])
        out_ref[half * 16 : half * 16 + 16, :] = (num / den).astype(bf16)

    for copy in started:
        copy.wait_send()


def body(query_nope, query_rope, cache_latent, cache_rope, key_weight, value_weight, span_starts):
    dma = pltpu.SemaphoreType.DMA
    vmem = pltpu.VMEM
    out = pl.pallas_call(
        kernel,
        out_shape=pltpu.VMEM((32, 128), bf16),
        in_specs=[pl.BlockSpec(memory_space=pltpu.SMEM)] + [pl.BlockSpec(memory_space=pl.ANY)] * 6,
        out_specs=pl.BlockSpec(memory_space=pltpu.VMEM),
        scratch_shapes=[
            vmem((1, 1, 4096), bf16), vmem((1, 1, 2048), bf16), vmem((2, 32, 128), f32), vmem((2, 32, 128), bf16),
            vmem((2, 2, 32, 128), bf16), vmem((2, 3, 16, 128), bf16), vmem((2, 16, 3, 16, 128), bf16), vmem((768, 128), f32),
            vmem((HEADS, 128, 512), bf16), vmem((HEADS, 512, 128), bf16),
            vmem((5, 256, 512), bf16), vmem((5, 2, 64, 128), bf16), vmem((128, 1280), bf16),
            vmem((2 * SIDE, 512), bf16), vmem((2 * SIDE, 128), bf16), vmem((2 * SIDE, 128), f32), vmem((2 * SIDE, 128), f32),
            vmem((2 * SIDE, 512), f32), vmem((768, 128), f32),
            vmem((2, 16, 48, 128), bf16), vmem((2, 16, 48, 128), bf16), vmem((2, 2, 32, 128), bf16), vmem((2, 2, 32, 128), bf16),
            dma((6,)), dma((2, 15)), dma((2, 15)), dma((3,)), dma((3,)), dma((3,)), dma((3,)), dma((4, PARTS)), dma((4, PARTS)),
            dma((5, PARTS)), dma((5, PARTS)), dma((2, 15)), dma((2, 15)),
        ],
        compiler_params=pltpu.CompilerParams(collective_id=0, has_side_effects=True, vmem_limit_bytes=63 << 20),
        cost_estimate=pl.CostEstimate(flops=2 * 1024 * 1024 * 1152, bytes_accessed=5 << 20, transcendentals=1 << 20),
    )(span_starts, query_nope, query_rope, cache_latent, jnp.swapaxes(cache_rope, 1, 2), key_weight, value_weight)
    return out.reshape(1, 1, 4096)


def solution(mesh):
    placed = (
        P(None, "seq", "head"),
        P(None, "seq", "head"),
        P(None, ("seq", "head"), None),
        P(None, ("seq", "head"), None),
        P("head", None, None),
        P("head", None, None),
        P(),
    )
    return jax.shard_map(
        body, mesh=mesh, in_specs=placed, out_specs=P(None, "seq", "head"), check_vma=False
    )
```

```python
import jax
import jax.numpy as jnp
from jax import lax
from jax.experimental import pallas as pl
from jax.experimental.pallas import tpu as pltpu
from jax.sharding import PartitionSpec as P

MESH = pl.DeviceIdType.MESH
bf16, f32 = jnp.bfloat16, jnp.float32
gain = 0.13524
gain2 = gain * 1.4426950408889634
floor_value = -1e30

HEADS = 16
TOKENS = 32
SIDE = HEADS * TOKENS
BLOCK = 512
PARTS = 3
ORDER = sorted(
    ((dx, dy) for dx in range(4) for dy in range(4) if dx or dy), key=lambda d: -min(d[0], 4 - d[0]) - min(d[1], 4 - d[1])
)


def coords():
    s, zl = lax.axis_index("seq"), lax.axis_index("head")
    return s // 16, (s // 4) % 4, ((s // 2) % 2) * 4 + zl, s % 2


def device(x, y, z, c):
    return (((x * 4 + y) * 2 + z // 4) * 2 + c, z % 4)


def remote(src, dst, send, recv, to):
    return pltpu.make_async_remote_copy(src, dst, send, recv, device_id=to, device_id_type=MESH)


def split3(v):
    hi = v.astype(bf16).astype(f32)
    mid = (v - hi).astype(bf16).astype(f32)
    return hi, mid, v - hi - mid


def pack_stats(stats):
    lane = lax.broadcasted_iota(jnp.int32, (16, 128), 1)
    packed = jnp.zeros((16, 128), f32)
    for i, v in enumerate(part for stat in stats for part in split3(stat)):
        packed = jnp.where(lane == i, v, packed)
    return packed


def merge(parts):
    lane = lax.broadcasted_iota(jnp.int32, (16, 128), 1)
    tops, totals = [], []
    for _, stats, at in parts:
        stats = stats.astype(f32)
        tops.append(jnp.sum(jnp.where((lane >= at) & (lane < at + 3), stats, 0.0), axis=1, keepdims=True))
        totals.append(jnp.sum(jnp.where((lane >= at + 3) & (lane < at + 6), stats, 0.0), axis=1, keepdims=True))
    top = tops[0]
    for t in tops[1:]:
        top = jnp.maximum(top, t)
    num, den = jnp.zeros((16, 128), f32), jnp.zeros((16, 1), f32)
    for (sums, _, _), t, total in zip(parts, tops, totals):
        scale = jnp.exp2((t - top) * gain2)
        num += scale * sums.astype(f32)
        den += scale * total
    return num, top, den


def kernel(span_ref, qn_hbm, qr_hbm, lat_hbm, rope_hbm, kw_hbm, vw_hbm, out_ref,
           qn, qr, qtmp, qs, qc, qm, rq, qf, kw, vw, lat, rp, rx, a_lat, a_rope, m_s, l_s, acc, of, so, ro, mm, fin,
           load_sem, q_send, q_recv, z_send, z_recv, f_send, f_recv, r_send, r_recv, c_send, c_recv, o_send, o_recv):
    x, y, z, c = coords()
    up, down = device(x, y, (z + 1) % 8, c), device(x, y, (z + 7) % 8, c)
    far = [device(x, y, (z + 4) % 8, c), device(x, y, (z + 4) % 8, 1 - c)]
    other = device(x, y, z, 1 - c)
    me = x * 4 + y
    peers = []
    for dx, dy in ORDER:
        px, py = (x + dx) % 4, (y + dy) % 4
        peers.append((device(px, py, z, c), px * 4 + py))

    barrier = pltpu.get_barrier_semaphore()
    for to in far + [up, down, other] + [p[0] for p in peers]:
        pl.semaphore_signal(barrier, inc=1, device_id=to, device_id_type=MESH)

    rows_of = pl.ds(pl.multiple_of(c * 128, 128), 128)
    loads = [
        pltpu.make_async_copy(qn_hbm, qn, load_sem.at[0]),
        pltpu.make_async_copy(qr_hbm, qr, load_sem.at[1]),
        pltpu.make_async_copy(rope_hbm.at[0], rp.at[0, c], load_sem.at[2]),
        pltpu.make_async_copy(lat_hbm.at[0], lat.at[0, rows_of], load_sem.at[3]),
        pltpu.make_async_copy(kw_hbm.at[pl.ds(c * HEADS, HEADS)], kw, load_sem.at[4]),
        pltpu.make_async_copy(vw_hbm.at[pl.ds(c * HEADS, HEADS)], vw, load_sem.at[5]),
    ]
    for copy in loads:
        copy.start()

    loads[0].wait()
    loads[1].wait()
    qtmp[...] = jnp.zeros_like(qtmp)
    nope_row, rope_row = qn[0].astype(f32), qr[0].astype(f32)
    for half in range(2):
        for h in range(HEADS):
            at = (half * HEADS + h) * 128
            qtmp[half, h : h + 1, :] = nope_row[:, at : at + 128]
        for h in range(HEADS // 2):
            at = (half * HEADS // 2 + h) * 128
            qtmp[half, pl.ds(16 + 8 * c + h, 1), :] = rope_row[:, at : at + 128]
    qs[...] = qtmp[...].astype(bf16)
    loads[2].wait()
    loads[3].wait()

    pl.semaphore_wait(barrier, 20)

    started = []

    def start(copy):
        copy.start()
        started.append(copy)
        return copy

    def piece(slot, part):
        if part == 2:
            return rp.at[slot, c]
        return lat.at[slot, pl.ds(pl.multiple_of(c * 128 + 64 * part, 64), 64)]

    def pair(slot, part):
        ref = piece(slot, part)
        return start(remote(ref, ref, c_send.at[slot, part], c_recv.at[slot, part], other))

    to_far = [
        start(remote(qs.at[c], qc.at[1, c], z_send.at[0], z_recv.at[0], far[0])),
        start(remote(qs.at[1 - c], qc.at[1, c], z_send.at[1], z_recv.at[1], far[1])),
    ]
    to_other = start(remote(qs.at[1 - c], qc.at[0, c], z_send.at[2], z_recv.at[2], other))
    qc[0, c] = qs[c]
    hop1, hop2, paired = {}, {}, []
    for part in range(PARTS):
        for d, to in enumerate((up, down)):
            hop1[d, part] = start(
                remote(piece(0, part), piece(1 + d, part), r_send.at[d, part], r_recv.at[d, part], to)
            )

    def send_queries(side):
        for core in range(2):
            qm[side, core] = qc[side, core, 0:16, :]
        qm[side, 2] = qc[side, 0, 16:32, :] + qc[side, 1, 16:32, :]
        copies = []
        for i, (to, _) in enumerate(peers):
            copies.append(start(remote(qm.at[side], rq.at[side, me], q_send.at[side, i], q_recv.at[side, i], to)))
        rq[side, me] = qm[side]
        return copies

    for part in range(PARTS):
        paired.append(pair(0, part))
    to_other.wait_recv()
    own_queries = send_queries(0)

    def arrive(part):
        for d in range(2):
            hop1[d, part].wait_recv()
            hop2[d, part] = start(
                remote(piece(1 + d, part), piece(3 + d, part), r_send.at[2 + d, part], r_recv.at[2 + d, part], (up, down)[d])
            )
        for d in range(2):
            paired.append(pair(1 + d, part))

    for copy in to_far:
        copy.wait_recv()
    far_queries = send_queries(1)
    for part in range(PARTS):
        arrive(part)

    lane_t = lax.broadcasted_iota(jnp.int32, (TOKENS, 128), 1)

    def by_head(row):
        return [qf[pl.ds(row[core], 16, stride=48), :] for core in range(2)]

    def absorb(side):
        qf[...] = rq[side].reshape(16 * 48, 128).astype(f32)
        for h in range(HEADS):
            rows = slice(side * SIDE + h * TOKENS, side * SIDE + (h + 1) * TOKENS)
            nope = jnp.concatenate(by_head((h, 16 + h)), axis=0).astype(bf16)
            a_lat[rows, :] = jnp.dot(nope, kw[h], preferred_element_type=f32).astype(bf16)
            rope = jnp.concatenate(by_head((32 + h // 2, 40 + h // 2)), axis=0)
            a_rope[rows, :] = jnp.where((lane_t < 64) == (h % 2 == 0), rope, 0.0).astype(bf16)

    def double_keys(slot):
        for cc in range(2):
            for twice in range(2):
                at = 256 * slot + 128 * cc
                rx[64 * twice : 64 * twice + 64, at : at + 128] = rp[slot, cc]

    row = lax.broadcasted_iota(jnp.int32, (BLOCK, 128), 0) % TOKENS
    column = lax.broadcasted_iota(jnp.int32, (BLOCK, 128), 1)

    def attend(side, block, low, high, first):
        rows = pl.ds(side * SIDE + block * BLOCK, BLOCK)
        z_hi = (z // 4 + side) % 2
        limit = span_ref[0] + (row % 16) * 4 + z_hi * 2 + row // 16 - column
        keys = lat[low:high].reshape((high - low) * 256, 512)
        s = lax.dot_general(a_lat[rows, :], keys, (((1,), (1,)), ((), ())), preferred_element_type=f32)
        s += jnp.dot(a_rope[rows, :], rx[:, 256 * low : 256 * high], preferred_element_type=f32)
        tiles = []
        for slot in range(low, high):
            for cc in range(2):
                zz = (z + (0, 7, 1, 6, 2)[slot]) % 8
                base = ((((x * 4 + y) * 2 + zz // 4) * 2 + cc) * 4 + zz % 4) * 128
                at = 128 * len(tiles)
                tiles.append(jnp.where(limit >= base, s[:, at : at + 128], floor_value))
        top = tiles[0]
        for tile in tiles[1:]:
            top = jnp.maximum(top, tile)
        top = jnp.broadcast_to(jnp.max(top, axis=1, keepdims=True), (BLOCK, 128))
        if not first:
            before = m_s[rows, :]
            top = jnp.maximum(top, before)
            keep = jnp.exp2((before - top) * gain2)
        mass = [jnp.exp2((tile - top) * gain2) for tile in tiles]
        total = mass[0]
        for tile in mass[1:]:
            total = total + tile
        total = jnp.broadcast_to(jnp.sum(total, axis=1, keepdims=True), (BLOCK, 128))
        update = jnp.dot(jnp.concatenate(mass, axis=1).astype(bf16), keys, preferred_element_type=f32)
        m_s[rows, :] = top
        if first:
            l_s[rows, :] = total
            acc[rows, :] = update
        else:
            l_s[rows, :] = l_s[rows, :] * keep + total
            for t in range(4):
                at = slice(128 * t, 128 * t + 128)
                acc[rows, at] = acc[rows, at] * keep + update[:, at]

    def send_partials(side):
        for h in range(HEADS):
            rows = slice(side * SIDE + h * TOKENS, side * SIDE + (h + 1) * TOKENS)
            result = jnp.dot(acc[rows, :].astype(bf16), vw[h], preferred_element_type=f32)
            stats = []
            for core in range(2):
                of[pl.ds(16 * core + h, 16, stride=48), :] = result[16 * core : 16 * core + 16]
                at = slice(rows.start + 16 * core, rows.start + 16 * core + 16)
                stats += [m_s[at, :], l_s[at, :]]
            of[pl.ds(32 + h, 16, stride=48), :] = pack_stats(stats)
        so[side] = of[...].reshape(16, 48, 128).astype(bf16)
        copies = []
        for i, (to, p) in enumerate(peers):
            copies.append(
                start(remote(so.at[side, p], ro.at[side, me], o_send.at[side, i], o_recv.at[side, i], to))
            )
        ro[side, me] = so[side, me]
        return copies

    loads[4].wait()
    for copy in own_queries:
        copy.wait_recv()
    absorb(0)
    for copy in paired:
        copy.wait_recv()
    for slot in range(3):
        double_keys(slot)
    for block in range(SIDE // BLOCK):
        attend(0, block, 0, 3, True)

    for copy in far_queries:
        copy.wait_recv()
    absorb(1)
    for block in range(SIDE // BLOCK):
        attend(1, block, 0, 3, True)
    last = []
    for part in range(PARTS):
        for d in range(2):
            hop2[d, part].wait_recv()
            last.append(pair(3 + d, part))
    loads[5].wait()
    far_partials = send_partials(1)
    for copy in last:
        copy.wait_recv()
    for slot in (3, 4):
        double_keys(slot)
    for block in range(SIDE // BLOCK):
        attend(0, block, 3, 5, False)
    early = list(started)
    own_partials = send_partials(0)
    for copy in early:
        copy.wait_send()

    def merge_plane(side):
        for core in range(2):
            num, top, den = merge(
                [(ro[side, p, 16 * core : 16 * core + 16, :], ro[side, p, 32:48, :], 6 * core) for p in range(16)]
            )
            mm[side, core, 0:16, :] = num.astype(bf16)
            mm[side, core, 16:32, :] = pack_stats([top, den]).astype(bf16)

    for copy in far_partials:
        copy.wait_recv()
    merge_plane(1)
    finals = [
        start(remote(mm.at[1, c], fin.at[1, c], f_send.at[0], f_recv.at[0], far[0])),
        start(remote(mm.at[1, 1 - c], fin.at[1, c], f_send.at[1], f_recv.at[1], far[1])),
    ]
    for copy in own_partials:
        copy.wait_recv()
    merge_plane(0)
    finals.append(start(remote(mm.at[0, 1 - c], fin.at[0, c], f_send.at[2], f_recv.at[2], other)))
    fin[0, c] = mm[0, c]
    for copy in own_partials:
        copy.wait_send()
    for copy in finals:
        copy.wait_recv()
    for half in range(2):
        num, _, den = merge([(fin[source, half, 0:16, :], fin[source, half, 16:32, :], 0) for source in range(2)])
        out_ref[half * 16 : half * 16 + 16, :] = (num / den).astype(bf16)

    for copy in finals:
        copy.wait_send()


def body(query_nope, query_rope, cache_latent, cache_rope, key_weight, value_weight, span_starts):
    dma = pltpu.SemaphoreType.DMA
    vmem = pltpu.VMEM
    out = pl.pallas_call(
        kernel,
        out_shape=pltpu.VMEM((32, 128), bf16),
        in_specs=[pl.BlockSpec(memory_space=pltpu.SMEM)] + [pl.BlockSpec(memory_space=pl.ANY)] * 6,
        out_specs=pl.BlockSpec(memory_space=pltpu.VMEM),
        scratch_shapes=[
            vmem((1, 1, 4096), bf16), vmem((1, 1, 2048), bf16), vmem((2, 32, 128), f32), vmem((2, 32, 128), bf16),
            vmem((2, 2, 32, 128), bf16), vmem((2, 3, 16, 128), bf16), vmem((2, 16, 3, 16, 128), bf16), vmem((768, 128), f32),
            vmem((HEADS, 128, 512), bf16), vmem((HEADS, 512, 128), bf16),
            vmem((5, 256, 512), bf16), vmem((5, 2, 64, 128), bf16), vmem((128, 1280), bf16),
            vmem((2 * SIDE, 512), bf16), vmem((2 * SIDE, 128), bf16), vmem((2 * SIDE, 128), f32), vmem((2 * SIDE, 128), f32),
            vmem((2 * SIDE, 512), f32), vmem((768, 128), f32),
            vmem((2, 16, 48, 128), bf16), vmem((2, 16, 48, 128), bf16), vmem((2, 2, 32, 128), bf16), vmem((2, 2, 32, 128), bf16),
            dma((6,)), dma((2, 15)), dma((2, 15)), dma((3,)), dma((3,)), dma((3,)), dma((3,)), dma((4, PARTS)), dma((4, PARTS)),
            dma((5, PARTS)), dma((5, PARTS)), dma((2, 15)), dma((2, 15)),
        ],
        compiler_params=pltpu.CompilerParams(collective_id=0, has_side_effects=True, vmem_limit_bytes=63 << 20),
        cost_estimate=pl.CostEstimate(flops=2 * 1024 * 1024 * 1152, bytes_accessed=5 << 20, transcendentals=1 << 20),
    )(span_starts, query_nope, query_rope, cache_latent, jnp.swapaxes(cache_rope, 1, 2), key_weight, value_weight)
    return out.reshape(1, 1, 4096)


def solution(mesh):
    placed = (
        P(None, "seq", "head"),
        P(None, "seq", "head"),
        P(None, ("seq", "head"), None),
        P(None, ("seq", "head"), None),
        P("head", None, None),
        P("head", None, None),
        P(),
    )
    return jax.shard_map(
        body, mesh=mesh, in_specs=placed, out_specs=P(None, "seq", "head"), check_vma=False
    )
```

```python
import jax
import jax.numpy as jnp
from jax import lax
from jax.experimental import pallas as pl
from jax.experimental.pallas import tpu as pltpu
from jax.sharding import PartitionSpec as P

MESH = pl.DeviceIdType.MESH
bf16, f32 = jnp.bfloat16, jnp.float32
gain = 0.13524
gain2 = gain * 1.4426950408889634
floor_value = -1e30

HEADS = 16
TOKENS = 32
SIDE = HEADS * TOKENS
BLOCK = 512
PARTS = 3
ORDER = sorted(
    ((dx, dy) for dx in range(4) for dy in range(4) if dx or dy), key=lambda d: -min(d[0], 4 - d[0]) - min(d[1], 4 - d[1])
)


def coords():
    s, zl = lax.axis_index("seq"), lax.axis_index("head")
    return s // 16, (s // 4) % 4, ((s // 2) % 2) * 4 + zl, s % 2


def device(x, y, z, c):
    return (((x * 4 + y) * 2 + z // 4) * 2 + c, z % 4)


def remote(src, dst, send, recv, to):
    return pltpu.make_async_remote_copy(src, dst, send, recv, device_id=to, device_id_type=MESH)


def split3(v):
    hi = v.astype(bf16).astype(f32)
    mid = (v - hi).astype(bf16).astype(f32)
    return hi, mid, v - hi - mid


def pack_stats(stats):
    lane = lax.broadcasted_iota(jnp.int32, (16, 128), 1)
    packed = jnp.zeros((16, 128), f32)
    for i, v in enumerate(part for stat in stats for part in split3(stat)):
        packed = jnp.where(lane == i, v, packed)
    return packed


def merge(parts):
    lane = lax.broadcasted_iota(jnp.int32, (16, 128), 1)
    tops, totals = [], []
    for _, stats, at in parts:
        stats = stats.astype(f32)
        tops.append(jnp.sum(jnp.where((lane >= at) & (lane < at + 3), stats, 0.0), axis=1, keepdims=True))
        totals.append(jnp.sum(jnp.where((lane >= at + 3) & (lane < at + 6), stats, 0.0), axis=1, keepdims=True))
    top = tops[0]
    for t in tops[1:]:
        top = jnp.maximum(top, t)
    num, den = jnp.zeros((16, 128), f32), jnp.zeros((16, 1), f32)
    for (sums, _, _), t, total in zip(parts, tops, totals):
        scale = jnp.exp2((t - top) * gain2)
        num += scale * sums.astype(f32)
        den += scale * total
    return num, top, den


def kernel(span_ref, qn_hbm, qr_hbm, lat_hbm, rope_hbm, kw_hbm, vw_hbm, out_ref,
           qn, qr, qtmp, qs, qc, qm, rq, qf, kw, vw, lat, rp, rx, a_lat, a_rope, m_s, l_s, acc, of, so, ro, mm, fin,
           load_sem, q_send, q_recv, z_send, z_recv, f_send, f_recv, r_send, r_recv, c_send, c_recv, o_send, o_recv):
    x, y, z, c = coords()
    up, down = device(x, y, (z + 1) % 8, c), device(x, y, (z + 7) % 8, c)
    far = [device(x, y, (z + 4) % 8, c), device(x, y, (z + 4) % 8, 1 - c)]
    other = device(x, y, z, 1 - c)
    me = x * 4 + y
    peers = []
    for dx, dy in ORDER:
        px, py = (x + dx) % 4, (y + dy) % 4
        peers.append((device(px, py, z, c), px * 4 + py))

    barrier = pltpu.get_barrier_semaphore()
    for to in far + [up, down, other] + [p[0] for p in peers]:
        pl.semaphore_signal(barrier, inc=1, device_id=to, device_id_type=MESH)

    rows_of = pl.ds(pl.multiple_of(c * 128, 128), 128)
    loads = [
        pltpu.make_async_copy(qn_hbm, qn, load_sem.at[0]),
        pltpu.make_async_copy(qr_hbm, qr, load_sem.at[1]),
        pltpu.make_async_copy(rope_hbm.at[0], rp.at[0, c], load_sem.at[2]),
        pltpu.make_async_copy(lat_hbm.at[0], lat.at[0, rows_of], load_sem.at[3]),
        pltpu.make_async_copy(kw_hbm.at[pl.ds(c * HEADS, HEADS)], kw, load_sem.at[4]),
        pltpu.make_async_copy(vw_hbm.at[pl.ds(c * HEADS, HEADS)], vw, load_sem.at[5]),
    ]
    for copy in loads:
        copy.start()

    loads[0].wait()
    loads[1].wait()
    qtmp[...] = jnp.zeros_like(qtmp)
    nope_row, rope_row = qn[0].astype(f32), qr[0].astype(f32)
    for half in range(2):
        for h in range(HEADS):
            at = (half * HEADS + h) * 128
            qtmp[half, h : h + 1, :] = nope_row[:, at : at + 128]
        for h in range(HEADS // 2):
            at = (half * HEADS // 2 + h) * 128
            qtmp[half, pl.ds(16 + 8 * c + h, 1), :] = rope_row[:, at : at + 128]
    qs[...] = qtmp[...].astype(bf16)
    loads[2].wait()
    loads[3].wait()

    pl.semaphore_wait(barrier, 20)

    started = []

    def start(copy):
        copy.start()
        started.append(copy)
        return copy

    def piece(slot, part):
        if part == 2:
            return rp.at[slot, c]
        return lat.at[slot, pl.ds(pl.multiple_of(c * 128 + 64 * part, 64), 64)]

    def pair(slot, part):
        ref = piece(slot, part)
        return start(remote(ref, ref, c_send.at[slot, part], c_recv.at[slot, part], other))

    to_far = [
        start(remote(qs.at[c], qc.at[1, c], z_send.at[0], z_recv.at[0], far[0])),
        start(remote(qs.at[1 - c], qc.at[1, c], z_send.at[1], z_recv.at[1], far[1])),
    ]
    to_other = start(remote(qs.at[1 - c], qc.at[0, c], z_send.at[2], z_recv.at[2], other))
    qc[0, c] = qs[c]
    hop1, hop2, paired = {}, {}, []
    for part in range(PARTS):
        for d, to in enumerate((up, down)):
            hop1[d, part] = start(
                remote(piece(0, part), piece(1 + d, part), r_send.at[d, part], r_recv.at[d, part], to)
            )

    def send_queries(side):
        for core in range(2):
            qm[side, core] = qc[side, core, 0:16, :]
        qm[side, 2] = qc[side, 0, 16:32, :] + qc[side, 1, 16:32, :]
        copies = []
        for i, (to, _) in enumerate(peers):
            copies.append(start(remote(qm.at[side], rq.at[side, me], q_send.at[side, i], q_recv.at[side, i], to)))
        rq[side, me] = qm[side]
        return copies

    for part in range(PARTS):
        paired.append(pair(0, part))
    to_other.wait_recv()
    own_queries = send_queries(0)

    def arrive(part):
        for d in range(2):
            hop1[d, part].wait_recv()
            hop2[d, part] = start(
                remote(piece(1 + d, part), piece(3 + d, part), r_send.at[2 + d, part], r_recv.at[2 + d, part], (up, down)[d])
            )
        for d in range(2):
            paired.append(pair(1 + d, part))

    for copy in to_far:
        copy.wait_recv()
    far_queries = send_queries(1)
    for part in range(PARTS):
        arrive(part)

    lane_t = lax.broadcasted_iota(jnp.int32, (TOKENS, 128), 1)

    def by_head(row):
        return [qf[pl.ds(row[core], 16, stride=48), :] for core in range(2)]

    def absorb(side):
        qf[...] = rq[side].reshape(16 * 48, 128).astype(f32)
        for h in range(HEADS):
            rows = slice(side * SIDE + h * TOKENS, side * SIDE + (h + 1) * TOKENS)
            nope = jnp.concatenate(by_head((h, 16 + h)), axis=0).astype(bf16)
            a_lat[rows, :] = jnp.dot(nope, kw[h], preferred_element_type=f32).astype(bf16)
            rope = jnp.concatenate(by_head((32 + h // 2, 40 + h // 2)), axis=0)
            a_rope[rows, :] = jnp.where((lane_t < 64) == (h % 2 == 0), rope, 0.0).astype(bf16)

    def double_keys(slot):
        for cc in range(2):
            for twice in range(2):
                at = 256 * slot + 128 * cc
                rx[64 * twice : 64 * twice + 64, at : at + 128] = rp[slot, cc]

    row = lax.broadcasted_iota(jnp.int32, (BLOCK, 128), 0) % TOKENS
    column = lax.broadcasted_iota(jnp.int32, (BLOCK, 128), 1)

    def attend(side, block, low, high, first):
        rows = pl.ds(side * SIDE + block * BLOCK, BLOCK)
        z_hi = (z // 4 + side) % 2
        limit = span_ref[0] + (row % 16) * 4 + z_hi * 2 + row // 16 - column
        keys = lat[low:high].reshape((high - low) * 256, 512)
        s = lax.dot_general(a_lat[rows, :], keys, (((1,), (1,)), ((), ())), preferred_element_type=f32)
        s += jnp.dot(a_rope[rows, :], rx[:, 256 * low : 256 * high], preferred_element_type=f32)
        tiles = []
        for slot in range(low, high):
            for cc in range(2):
                zz = (z + (0, 7, 1, 6, 2)[slot]) % 8
                base = ((((x * 4 + y) * 2 + zz // 4) * 2 + cc) * 4 + zz % 4) * 128
                at = 128 * len(tiles)
                tiles.append(jnp.where(limit >= base, s[:, at : at + 128], floor_value))
        top = tiles[0]
        for tile in tiles[1:]:
            top = jnp.maximum(top, tile)
        top = jnp.broadcast_to(jnp.max(top, axis=1, keepdims=True), (BLOCK, 128))
        if not first:
            before = m_s[rows, :]
            top = jnp.maximum(top, before)
            keep = jnp.exp2((before - top) * gain2)
        mass = [jnp.exp2((tile - top) * gain2) for tile in tiles]
        total = mass[0]
        for tile in mass[1:]:
            total = total + tile
        total = jnp.broadcast_to(jnp.sum(total, axis=1, keepdims=True), (BLOCK, 128))
        update = jnp.dot(jnp.concatenate(mass, axis=1).astype(bf16), keys, preferred_element_type=f32)
        m_s[rows, :] = top
        if first:
            l_s[rows, :] = total
            acc[rows, :] = update
        else:
            l_s[rows, :] = l_s[rows, :] * keep + total
            for t in range(4):
                at = slice(128 * t, 128 * t + 128)
                acc[rows, at] = acc[rows, at] * keep + update[:, at]

    def send_partials(side):
        for h in range(HEADS):
            rows = slice(side * SIDE + h * TOKENS, side * SIDE + (h + 1) * TOKENS)
            result = jnp.dot(acc[rows, :].astype(bf16), vw[h], preferred_element_type=f32)
            stats = []
            for core in range(2):
                of[pl.ds(16 * core + h, 16, stride=48), :] = result[16 * core : 16 * core + 16]
                at = slice(rows.start + 16 * core, rows.start + 16 * core + 16)
                stats += [m_s[at, :], l_s[at, :]]
            of[pl.ds(32 + h, 16, stride=48), :] = pack_stats(stats)
        copies = []
        for i, (to, p) in enumerate(peers):
            so[side, p] = of[pl.ds(pl.multiple_of(48 * p, 16), 48), :].astype(bf16)
            copies.append(
                start(remote(so.at[side, p], ro.at[side, me], o_send.at[side, i], o_recv.at[side, i], to))
            )
        ro[side, me] = of[pl.ds(pl.multiple_of(48 * me, 16), 48), :].astype(bf16)
        return copies

    loads[4].wait()
    for copy in own_queries:
        copy.wait_recv()
    absorb(0)
    for copy in paired:
        copy.wait_recv()
    for slot in range(3):
        double_keys(slot)
    for block in range(SIDE // BLOCK):
        attend(0, block, 0, 3, True)

    for copy in far_queries:
        copy.wait_recv()
    absorb(1)
    for block in range(SIDE // BLOCK):
        attend(1, block, 0, 3, True)
    last = []
    for part in range(PARTS):
        for d in range(2):
            hop2[d, part].wait_recv()
            last.append(pair(3 + d, part))
    loads[5].wait()
    far_partials = send_partials(1)
    for copy in last:
        copy.wait_recv()
    for slot in (3, 4):
        double_keys(slot)
    for block in range(SIDE // BLOCK):
        attend(0, block, 3, 5, False)
    early = list(started)
    own_partials = send_partials(0)
    for copy in early:
        copy.wait_send()

    def merge_plane(side):
        for core in range(2):
            num, top, den = merge(
                [(ro[side, p, 16 * core : 16 * core + 16, :], ro[side, p, 32:48, :], 6 * core) for p in range(16)]
            )
            mm[side, core, 0:16, :] = num.astype(bf16)
            mm[side, core, 16:32, :] = pack_stats([top, den]).astype(bf16)

    for copy in far_partials:
        copy.wait_recv()
    merge_plane(1)
    finals = [
        start(remote(mm.at[1, c], fin.at[1, c], f_send.at[0], f_recv.at[0], far[0])),
        start(remote(mm.at[1, 1 - c], fin.at[1, c], f_send.at[1], f_recv.at[1], far[1])),
    ]
    for copy in own_partials:
        copy.wait_recv()
    merge_plane(0)
    finals.append(start(remote(mm.at[0, 1 - c], fin.at[0, c], f_send.at[2], f_recv.at[2], other)))
    fin[0, c] = mm[0, c]
    for copy in own_partials:
        copy.wait_send()
    for copy in finals:
        copy.wait_recv()
    for half in range(2):
        num, _, den = merge([(fin[source, half, 0:16, :], fin[source, half, 16:32, :], 0) for source in range(2)])
        out_ref[half * 16 : half * 16 + 16, :] = (num / den).astype(bf16)

    for copy in finals:
        copy.wait_send()


def body(query_nope, query_rope, cache_latent, cache_rope, key_weight, value_weight, span_starts):
    dma = pltpu.SemaphoreType.DMA
    vmem = pltpu.VMEM
    out = pl.pallas_call(
        kernel,
        out_shape=pltpu.VMEM((32, 128), bf16),
        in_specs=[pl.BlockSpec(memory_space=pltpu.SMEM)] + [pl.BlockSpec(memory_space=pl.ANY)] * 6,
        out_specs=pl.BlockSpec(memory_space=pltpu.VMEM),
        scratch_shapes=[
            vmem((1, 1, 4096), bf16), vmem((1, 1, 2048), bf16), vmem((2, 32, 128), f32), vmem((2, 32, 128), bf16),
            vmem((2, 2, 32, 128), bf16), vmem((2, 3, 16, 128), bf16), vmem((2, 16, 3, 16, 128), bf16), vmem((768, 128), f32),
            vmem((HEADS, 128, 512), bf16), vmem((HEADS, 512, 128), bf16),
            vmem((5, 256, 512), bf16), vmem((5, 2, 64, 128), bf16), vmem((128, 1280), bf16),
            vmem((2 * SIDE, 512), bf16), vmem((2 * SIDE, 128), bf16), vmem((2 * SIDE, 128), f32), vmem((2 * SIDE, 128), f32),
            vmem((2 * SIDE, 512), f32), vmem((768, 128), f32),
            vmem((2, 16, 48, 128), bf16), vmem((2, 16, 48, 128), bf16), vmem((2, 2, 32, 128), bf16), vmem((2, 2, 32, 128), bf16),
            dma((6,)), dma((2, 15)), dma((2, 15)), dma((3,)), dma((3,)), dma((3,)), dma((3,)), dma((4, PARTS)), dma((4, PARTS)),
            dma((5, PARTS)), dma((5, PARTS)), dma((2, 15)), dma((2, 15)),
        ],
        compiler_params=pltpu.CompilerParams(collective_id=0, has_side_effects=True, vmem_limit_bytes=63 << 20),
        cost_estimate=pl.CostEstimate(flops=2 * 1024 * 1024 * 1152, bytes_accessed=5 << 20, transcendentals=1 << 20),
    )(span_starts, query_nope, query_rope, cache_latent, jnp.swapaxes(cache_rope, 1, 2), key_weight, value_weight)
    return out.reshape(1, 1, 4096)


def solution(mesh):
    placed = (
        P(None, "seq", "head"),
        P(None, "seq", "head"),
        P(None, ("seq", "head"), None),
        P(None, ("seq", "head"), None),
        P("head", None, None),
        P("head", None, None),
        P(),
    )
    return jax.shard_map(
        body, mesh=mesh, in_specs=placed, out_specs=P(None, "seq", "head"), check_vma=False
    )
```
